256 devices in a mesh: dp: 16 (over y, x_lo, core), seq: 16 (over x_hi, z).
Axes of the slice: x: 4 (x_hi: 2, x_lo: 2; x = x_hi * 2 + x_lo), y: 4, z: 8, core: 2. Of those that a mesh axis runs over, the one named last changes fastest.
Arguments:
- tokens: bfloat16 [16, 2048, 4096], P('dp', 'seq'), may hold values from -100 to 100
- query_weight: bfloat16 [4096, 4096], P('dp', 'seq'), may hold values from -0.09375 to 0.09375
- key_weight: bfloat16 [4096, 4096], P('dp', 'seq'), may hold values from -0.09375 to 0.09375
- value_weight: bfloat16 [4096, 4096], P('dp', 'seq'), may hold values from -0.09375 to 0.09375
- log_decay: float32 [16, 32, 2048], P('dp', 'seq'), may hold values from -0.75 to 0
Outputs:
- mixed: bfloat16 [16, 2048, 4096], P('dp', 'seq')
The draws below stay inside these ranges and needn't reach their ends.
All inputs are finite; a program needn't handle non-finite values.
Results may differ from the reference program's by a relative error of at most 0.0073.
Values may be sent and summed in bfloat16 or wider, within the bound.
No kernel may reach another device: no remote copies, remote signals or barrier semaphores. Data moves between devices by JAX's collectives and lax.ppermute only.
A program may use at most 128 MiB of HBM per device.

```python
import jax
import jax.numpy as jnp
from jax import lax

D = 4096
HEAD_TOTAL = 32
DH = 128
BLOCK = 256
SEQUENCE_TOTAL = 16
SEQUENCE_LENGTH = 2048


def draw_tokens(key, part):
    key = jax.random.fold_in(key, 11)
    key_collection = jax.random.split(key, 2)
    column_scale = jnp.exp(jax.random.uniform(key_collection[0], (D,), jnp.float32, jnp.log(0.3), jnp.log(3.0)))
    sampled_values = jax.random.normal(key_collection[1], (SEQUENCE_TOTAL, SEQUENCE_LENGTH, D), jnp.float32) * column_scale
    return jnp.clip(sampled_values, -100.0, 100.0).astype(jnp.bfloat16)


def draw_log_decay(key, part):
    key = jax.random.fold_in(key, 23)
    key_collection = jax.random.split(key, 6)
    fast_share = 0.5
    picked = jax.random.uniform(key_collection[0], (SEQUENCE_TOTAL, HEAD_TOTAL, 1), jnp.float32) < fast_share
    fast_rate = 1.0 / jax.random.uniform(key_collection[1], (SEQUENCE_TOTAL, HEAD_TOTAL, 1), jnp.float32, 30.0, 50.0)
    slow_rate = jax.random.uniform(key_collection[2], (SEQUENCE_TOTAL, HEAD_TOTAL, 1), jnp.float32, 0.1, 0.6) / SEQUENCE_LENGTH
    decay_rate = jnp.where(picked, fast_rate, slow_rate)
    coarse_estimate = jax.random.uniform(key_collection[3], (SEQUENCE_TOTAL, HEAD_TOTAL, SEQUENCE_LENGTH), jnp.float32, 0.5, 1.5)
    sudden_spike = jax.random.uniform(key_collection[4], (SEQUENCE_TOTAL, HEAD_TOTAL, SEQUENCE_LENGTH), jnp.float32) < 2.0 / SEQUENCE_LENGTH
    retained_rows = jax.random.uniform(key_collection[5], (SEQUENCE_TOTAL, HEAD_TOTAL, SEQUENCE_LENGTH), jnp.float32, 0.5, 0.8)
    sampled_values = -decay_rate * coarse_estimate + jnp.where(sudden_spike, jnp.log(retained_rows), 0.0)
    return sampled_values.astype(jnp.float32)


def level_of(rng, dims, pieces, low, largest):
    gain = 1.0
    for position, shards_of in pieces:
        draws = jax.random.uniform(jax.random.fold_in(jax.random.fold_in(rng, 6), position), (shards_of,), jnp.float32, low / len(pieces), largest / len(pieces))
        gain = gain * jnp.repeat(jnp.exp(draws), dims[position] // shards_of).reshape((-1,) + (1,) * (len(dims) - 1 - position))
    return gain


def bell_draw(rng, extent, scale, most, pieces=(), kind=jnp.bfloat16):
    loudness = level_of(rng, extent, pieces, -0.22, 0.18) if pieces else 1.0
    values = jax.random.normal(rng, extent, jnp.float32) * scale * loudness
    return jnp.minimum(jnp.maximum(values, -most), most).astype(kind)


def setup_inputs(seed: int = 0) -> dict:
    arg_keys = jax.random.split(jax.random.key(seed), 6)
    tokens = draw_tokens(jax.random.fold_in(arg_keys[5], 71), 0)
    query_weight = bell_draw(arg_keys[1], (D, HEAD_TOTAL * DH), D ** -0.5, 0.09375, ((0, 16), (1, 16)))
    key_weight = bell_draw(arg_keys[2], (D, HEAD_TOTAL * DH), D ** -0.5, 0.09375, ((0, 16), (1, 16)))
    value_weight = bell_draw(arg_keys[3], (D, HEAD_TOTAL * DH), D ** -0.5, 0.09375, ((0, 16), (1, 16)))
    log_decay = draw_log_decay(jax.random.fold_in(arg_keys[5], 71), 0)
    return dict(tokens=tokens, query_weight=query_weight, key_weight=key_weight, value_weight=value_weight, log_decay=log_decay)


def rounded(values_f):
    return lax.optimization_barrier(values_f.astype(jnp.bfloat16)).astype(jnp.float32)

def lightning(query, keys_in, values_in, log_decay, block_rows):
    length, head_count, head_width = query.shape
    block_count = length // block_rows
    queries = query.astype(jnp.float32).reshape(block_count, block_rows, head_count, head_width)
    keys_all = keys_in.astype(jnp.float32).reshape(block_count, block_rows, head_count, head_width)
    values_all = values_in.astype(jnp.float32).reshape(block_count, block_rows, head_count, head_width)
    log_gates = log_decay.astype(jnp.float32).reshape(head_count, block_count, block_rows).transpose(1, 0, 2)
    within = jnp.cumsum(log_gates, axis=-1)
    positions = jnp.arange(block_rows)
    causal = positions[:, None] >= positions[None, :]

    def advance(memory, blocks):
        query_block, key_block, value_block, decay_block = blocks
        scores = jnp.einsum('thd,shd->hts', query_block, key_block, precision=lax.Precision.HIGHEST)
        weights = jnp.where(causal[None], jnp.exp(decay_block[:, :, None] - decay_block[:, None, :]), 0.0)
        weighted = rounded(scores * weights)
        local_part = jnp.einsum('hts,shd->thd', weighted, value_block, precision=lax.Precision.HIGHEST)
        scaled_query = rounded(query_block * jnp.exp(decay_block).T[:, :, None])
        carried = jnp.einsum('thd,hde->the', scaled_query, rounded(memory), precision=lax.Precision.HIGHEST)
        block_total = decay_block[:, -1]
        fading = jnp.exp(block_total[:, None] - decay_block).T[:, :, None]
        faded_keys = rounded(key_block * fading)
        update = jnp.einsum('shd,she->hde', faded_keys, value_block, precision=lax.Precision.HIGHEST)
        memory = jnp.exp(block_total)[:, None, None] * memory + update
        return (memory, local_part + carried)
    initial = jnp.zeros((head_count, head_width, head_width), jnp.float32)
    final_memory, blocks_out = lax.scan(advance, initial, (queries, keys_all, values_all, within))
    attended = blocks_out.reshape(length, head_count, head_width)
    inverse_rms = lax.rsqrt(lax.optimization_barrier(jnp.mean(attended * attended, axis=-1, keepdims=True)) + 1e-06)
    return (attended * inverse_rms).astype(jnp.bfloat16).reshape(length, head_count * head_width)

def normalize_rows(token_rows):
    values_f = token_rows.astype(jnp.float32)
    inverse_rms = lax.rsqrt(lax.optimization_barrier(jnp.mean(values_f * values_f, axis=-1, keepdims=True)) + 1e-05)
    return (values_f * inverse_rms).astype(jnp.bfloat16)

def reference(tokens, query_weight, key_weight, value_weight, log_decay):

    def one_sequence(inputs):
        sequence_rows, sequence_decay = inputs
        normed = normalize_rows(sequence_rows)
        query = jax.nn.silu(jnp.dot(normed, query_weight, preferred_element_type=jnp.float32)).astype(jnp.bfloat16)
        keys_rows = jax.nn.silu(jnp.dot(normed, key_weight, preferred_element_type=jnp.float32)).astype(jnp.bfloat16)
        values_rows = jnp.dot(normed, value_weight, preferred_element_type=jnp.float32).astype(jnp.bfloat16)
        length = sequence_rows.shape[0]
        shaped = (length, HEAD_TOTAL, DH)
        return lightning(query.reshape(shaped), keys_rows.reshape(shaped), values_rows.reshape(shaped), sequence_decay, BLOCK)
    return lax.map(one_sequence, (tokens, log_decay))
```

```python
import jax
import jax.numpy as jnp
from jax import lax
from jax.experimental import pallas as pl
from jax.experimental.pallas import tpu as pltpu
from jax.sharding import Mesh, PartitionSpec as P

BLOCK = 256
DH = 128
SHAPE = (4, 2, 2, 2, 8)
NAMES = ("y", "xl", "c", "xh", "z")
X_INDEX = (0, 2, 1, 3)


def ring_y(value, step):
    return lax.ppermute(value, "y", [(i, (i + step) % 4) for i in range(4)])


def ring_x(value, step):
    return lax.ppermute(
        value, ("xl", "xh"), [(X_INDEX[i], X_INDEX[(i + step) % 4]) for i in range(4)]
    )


def swap_core(value):
    return lax.ppermute(value, "c", [(0, 1), (1, 0)])


def swap_half(value):
    return lax.ppermute(value, "xh", [(0, 1), (1, 0)])


def swap_roles(value):
    return lax.ppermute(value, ("c", "xh"), [(0, 0), (1, 2), (2, 1), (3, 3)])


def normalize_rows(token_rows):
    values_f = token_rows.astype(jnp.float32)
    inverse_rms = lax.rsqrt(jnp.mean(values_f * values_f, axis=-1, keepdims=True) + 1e-05)
    return (values_f * inverse_rms).astype(jnp.bfloat16)


def around(value, ring, axis):
    one, three = ring(value, 1), ring(value, -1)
    half = value.shape[axis] // 2
    first = lax.slice_in_dim(one, 0, half, axis=axis)
    second = lax.slice_in_dim(three, half, 2 * half, axis=axis)
    two = jnp.concatenate((ring(first, 1), ring(second, -1)), axis=axis)
    return jnp.stack((value, one, two, three))


def project_kernel(place_ref, rows_ref, weight_ref, *rest):
    out_ref = rest[-1]
    rows = rows_ref[0].reshape(rows_ref.shape[1] * rows_ref.shape[2], rows_ref.shape[3])
    for part in range(3):
        product = jnp.dot(
            rows, weight_ref[:, part * 256 : (part + 1) * 256], preferred_element_type=jnp.float32
        )
        if part < 2:
            product = product / (1.0 + jnp.exp(-product))
        out_ref[0, 0, :, :, part * 256 : (part + 1) * 256] = product.astype(jnp.bfloat16).reshape(
            out_ref.shape[2], out_ref.shape[3], 256
        )


def project(place, rows, weight, previous=None):
    group, width = 4, weight.shape[1]
    in_specs = [
        pl.BlockSpec((1, group, 64, rows.shape[3]), lambda i, j, place: (i, j, 0, 0)),
        pl.BlockSpec(weight.shape, lambda i, j, place: (0, 0)),
    ]
    operands = [rows, weight]
    aliases = {}
    if previous is not None:
        in_specs.append(pl.BlockSpec(memory_space=pl.ANY))
        operands.append(previous)
        aliases = {3: 0}
    return pl.pallas_call(
        project_kernel,
        out_shape=jax.ShapeDtypeStruct((2, 2, 8, 64, width), jnp.bfloat16),
        grid_spec=pltpu.PrefetchScalarGridSpec(
            num_scalar_prefetch=1,
            grid=(2, 8 // group),
            in_specs=in_specs,
            out_specs=pl.BlockSpec(
                (1, 1, group, 64, width), lambda i, j, place: (place[0], i, j, 0, 0)
            ),
        ),
        input_output_aliases=aliases,
        compiler_params=pltpu.CompilerParams(vmem_limit_bytes=48 << 20),
        cost_estimate=pl.CostEstimate(
            flops=2 * 1024 * 4096 * 768, bytes_accessed=16 << 20, transcendentals=0
        ),
        name="project",
    )(place, *operands)


def attend_kernel(qkv_ref, row_ref, column_ref, out_ref, state_ref):
    @pl.when(pl.program_id(0) == 0)
    def _():
        state_ref[...] = jnp.zeros_like(state_ref)

    def rows_of(start):
        part = qkv_ref[0, :, :, :, start : start + DH]
        return jnp.concatenate(
            [part[core, chunk] for chunk in range(2) for core in range(2)], axis=0
        )

    later = lax.broadcasted_iota(jnp.int32, (BLOCK, BLOCK), 0)
    earlier = lax.broadcasted_iota(jnp.int32, (BLOCK, BLOCK), 1)
    causal = later >= earlier
    for head in range(2):
        query = rows_of(head * DH)
        keys = rows_of(256 + head * DH)
        values = rows_of(512 + head * DH)
        g_row = row_ref[0, head : head + 1, :]
        g_column = column_ref[0, :, head : head + 1]
        total = g_row[:, BLOCK - 1 :]
        scores = lax.dot_general(
            query, keys, (((1,), (1,)), ((), ())), preferred_element_type=jnp.float32
        )
        weights = jnp.exp(jnp.where(causal, g_column - g_row, -jnp.inf))
        weighted = (scores * weights).astype(jnp.bfloat16)
        scaled_query = (query.astype(jnp.float32) * jnp.exp(g_column)).astype(jnp.bfloat16)
        state = state_ref[head]
        attended = jnp.dot(weighted, values, preferred_element_type=jnp.float32) + jnp.dot(
            scaled_query, state.astype(jnp.bfloat16), preferred_element_type=jnp.float32
        )
        faded_keys = (keys.astype(jnp.float32) * jnp.exp(total - g_column)).astype(jnp.bfloat16)
        update = lax.dot_general(
            faded_keys, values, (((0,), (0,)), ((), ())), preferred_element_type=jnp.float32
        )
        state_ref[head] = jnp.exp(total) * state + update
        inverse_rms = lax.rsqrt(jnp.mean(attended * attended, axis=-1, keepdims=True) + 1e-06)
        mixed = (attended * inverse_rms).astype(jnp.bfloat16)
        out_ref[:, :, head * DH : (head + 1) * DH] = mixed.reshape(2, BLOCK // 2, DH)


def attend(qkv, row, column):
    return pl.pallas_call(
        attend_kernel,
        out_shape=jax.ShapeDtypeStruct((16, 128, 256), jnp.bfloat16),
        grid_spec=pltpu.PrefetchScalarGridSpec(
            num_scalar_prefetch=0,
            grid=(8,),
            in_specs=[
                pl.BlockSpec((1, 2, 2, 64, 768), lambda i: (i // 4, 0, i % 4, 0, 0)),
                pl.BlockSpec((1, 2, BLOCK), lambda i: (i, 0, 0)),
                pl.BlockSpec((1, BLOCK, 2), lambda i: (i, 0, 0)),
            ],
            out_specs=pl.BlockSpec((2, 128, 256), lambda i: (i, 0, 0)),
            scratch_shapes=[pltpu.VMEM((2, DH, DH), jnp.float32)],
        ),
        compiler_params=pltpu.CompilerParams(vmem_limit_bytes=48 << 20),
        cost_estimate=pl.CostEstimate(
            flops=16 * 50_331_648, bytes_accessed=4 << 20, transcendentals=0
        ),
        name="attend",
    )(qkv, row, column)


def gather_weight(weight):
    y, half = lax.axis_index("y"), lax.axis_index("xh")
    x = half * 2 + lax.axis_index("xl")
    own = swap_roles(weight)
    by_row = own.reshape(2, 128, own.shape[1])
    first = around(around(by_row[0], ring_y, 0), ring_x, 1)
    second = around(around(by_row[1], ring_x, 0), ring_y, 1)
    both = jnp.stack((first.transpose(1, 0, 2, 3), second))
    order_y = jnp.mod(y - jnp.arange(4), 4)
    order_x = jnp.mod(x - jnp.arange(4), 4)
    both = jnp.take(jnp.take(both, order_y, axis=1), order_x, axis=2)
    both = both.reshape(2, 4, 2, 2, 128, weight.shape[1]).transpose(1, 3, 2, 0, 4, 5)
    return both.reshape(4096, weight.shape[1])


def shards(tokens, query_weight, key_weight, value_weight, log_decay):
    core, half = lax.axis_index("c"), lax.axis_index("xh")
    on_place = core == half
    normed = normalize_rows(tokens[0]).reshape(2, 64, 4096)
    kept = lax.dynamic_index_in_dim(normed, core, 0, keepdims=False)
    given = lax.dynamic_index_in_dim(normed, 1 - core, 0, keepdims=False)
    got = swap_core(given)
    staying = jnp.where(on_place, kept, got)
    leaving = jnp.where(on_place, got, kept)
    arrived = swap_half(leaving)
    near = lax.all_gather(staying, ("c", "z"), axis=0, tiled=False).reshape(2, 8, 64, 4096)
    far = lax.all_gather(arrived, ("c", "z"), axis=0, tiled=False).reshape(2, 8, 64, 4096)

    weight = gather_weight(jnp.concatenate((query_weight, key_weight, value_weight), axis=1))
    decay = swap_roles(log_decay[0])
    g = jnp.cumsum(decay.reshape(2, 8, BLOCK), axis=-1)
    row, column = g.transpose(1, 0, 2), g.transpose(1, 2, 0)

    place = half.astype(jnp.int32).reshape(1)
    qkv = project(place, near, weight)
    qkv = project(1 - place, far, weight, qkv)
    mixed = attend(qkv, row, column)
    spread = lax.all_to_all(mixed, ("c", "z"), split_axis=0, concat_axis=0, tiled=True)
    spread = swap_roles(spread)
    return spread.transpose(1, 0, 2).reshape(1, 128, 4096)


def solution(mesh):
    inner = Mesh(mesh.devices.reshape(SHAPE), NAMES)
    rows, lanes = ("y", "xl", "c"), ("xh", "z")
    placed = (
        P(rows, lanes, None),
        P(rows, lanes),
        P(rows, lanes),
        P(rows, lanes),
        P(rows, lanes, None),
    )
    return jax.shard_map(
        shards, mesh=inner, in_specs=placed, out_specs=P(rows, lanes, None), check_vma=False
    )
```

```python
import functools

import jax
import jax.numpy as jnp
from jax import lax
from jax.experimental import pallas as pl
from jax.experimental.pallas import tpu as pltpu
from jax.sharding import Mesh, PartitionSpec as P

BLOCK = 256
DH = 128
SHAPE = (4, 2, 2, 2, 8)
NAMES = ("y", "xl", "c", "xh", "z")


def swap_core(value):
    return lax.ppermute(value, "c", [(0, 1), (1, 0)])


def swap_half(value):
    return lax.ppermute(value, "xh", [(0, 1), (1, 0)])


def swap_roles(value):
    return lax.ppermute(value, ("c", "xh"), [(0, 0), (1, 2), (2, 1), (3, 3)])


def normalize_rows(token_rows):
    values_f = token_rows.astype(jnp.float32)
    inverse_rms = lax.rsqrt(jnp.mean(values_f * values_f, axis=-1, keepdims=True) + 1e-05)
    return (values_f * inverse_rms).astype(jnp.bfloat16)


def ring_z(value, step):
    return lax.ppermute(value, "z", [(i, (i + step) % 8) for i in range(8)])


def gather_weight(weight):
    order = [
        ((y * 2 + xl) * 2 + core) * 2 + xh
        for y in range(4)
        for xh in range(2)
        for xl in range(2)
        for core in range(2)
    ]
    whole = lax.all_gather(
        weight, ("y", "xl", "c", "xh"), axis=0, tiled=False, axis_index_groups=[order]
    )
    return whole.reshape(4, 2, 1024, weight.shape[1])


SLOTS = (
    [(0, 0), (1, 0), (0, 1), (0, 7), (0, 2), (0, 6), (1, 1), (1, 7)]
    + [(0, 3), (0, 5), (1, 2), (1, 6), (0, 4), (1, 3), (1, 5), (1, 4)]
)
BATCHES = ((0, 13), (13, 16))


def project_kernel(count, last_group, core_ref, *refs):
    pieces, weight_ref = refs[:count], refs[count]
    outs = refs[count + 1 :]
    group, part = pl.program_id(0), pl.program_id(1)
    rows = jnp.concatenate([piece[...] for piece in pieces], axis=0)
    weight = weight_ref[:, 0].reshape(4096, 256)
    product = jnp.dot(rows, weight, preferred_element_type=jnp.float32)
    gated = product / (1.0 + jnp.exp(-product))
    result = jnp.where(part < 2, gated, product).astype(jnp.bfloat16).reshape(-1, 64, 256)
    if last_group == 0:
        slots = outs[0].shape[0]
        outs[0][...] = result[:slots]
        outs[1][...] = result[slots:]
        return

    @pl.when(group == 0)
    def _():
        outs[0][...] = result

    @pl.when(group == 1)
    def _():
        outs[1][...] = result


def project(core, pieces, weight, both):
    rows = sum(piece.shape[0] for piece in pieces)
    width = weight.shape[3]
    groups = 2 if both else 1
    slots = rows // 64 if both else rows // 128
    out = jax.ShapeDtypeStruct((slots, 64, width), jnp.bfloat16)

    def columns(g, p, core):
        mine = 1 if not both else g
        return 0, mine * core[0] + (1 - mine) * (1 - core[0]), 0, p

    last = pl.BlockSpec((slots, 64, 256), lambda g, p, core: (0, 0, g * p))
    first = pl.BlockSpec((slots, 64, 256), lambda g, p, core: (0, 0, (1 - g) * p + g * 2))
    return pl.pallas_call(
        functools.partial(project_kernel, len(pieces), groups - 1),
        out_shape=(out, out),
        grid_spec=pltpu.PrefetchScalarGridSpec(
            num_scalar_prefetch=1,
            grid=(groups, 3),
            in_specs=[pl.BlockSpec(piece.shape, lambda g, p, core: (0, 0)) for piece in pieces]
            + [pl.BlockSpec((4, 1, 1024, 256), columns)],
            out_specs=[first, last if both else first],
        ),
        compiler_params=pltpu.CompilerParams(vmem_limit_bytes=58 << 20),
        cost_estimate=pl.CostEstimate(
            flops=groups * 2 * rows * 4096 * width,
            bytes_accessed=2 * rows * 8192 + groups * (6 << 20),
            transcendentals=0,
        ),
        name="project",
    )(core, *pieces, weight)


def attend_kernel(chunk_ref, core_ref, *refs):
    batches = len(BATCHES)
    kept, got = refs[:batches], refs[batches : 2 * batches]
    row_ref, column_ref, out_ref, all_ref = refs[2 * batches :]
    core = core_ref[0]
    for batch, (first, last) in enumerate(BATCHES):
        for slot in range(first, last):
            chunk = chunk_ref[slot]
            all_ref[chunk, core] = kept[batch][slot - first]
            all_ref[chunk, 1 - core] = got[batch][slot - first]
    later = lax.broadcasted_iota(jnp.int32, (BLOCK, BLOCK), 0)
    earlier = lax.broadcasted_iota(jnp.int32, (BLOCK, BLOCK), 1)
    causal = later >= earlier
    states = [jnp.zeros((DH, DH), jnp.float32)] * 2
    for step in range(8):
        rows = all_ref[2 * step : 2 * step + 2].reshape(BLOCK, 768)
        results = []
        for head in range(2):
            query = rows[:, head * DH : (head + 1) * DH]
            keys = rows[:, 256 + head * DH : 256 + (head + 1) * DH]
            values = rows[:, 512 + head * DH : 512 + (head + 1) * DH]
            g_row = row_ref[step, head : head + 1, :]
            g_column = column_ref[step, :, head : head + 1]
            total = g_row[:, BLOCK - 1 :]
            scores = lax.dot_general(
                query, keys, (((1,), (1,)), ((), ())), preferred_element_type=jnp.float32
            )
            weights = jnp.exp(jnp.where(causal, g_column - g_row, -jnp.inf))
            weighted = (scores * weights).astype(jnp.bfloat16)
            scaled_query = (query.astype(jnp.float32) * jnp.exp(g_column)).astype(jnp.bfloat16)
            state = states[head]
            attended = jnp.dot(weighted, values, preferred_element_type=jnp.float32) + jnp.dot(
                scaled_query, state.astype(jnp.bfloat16), preferred_element_type=jnp.float32
            )
            faded_keys = (keys.astype(jnp.float32) * jnp.exp(total - g_column)).astype(jnp.bfloat16)
            update = lax.dot_general(
                faded_keys, values, (((0,), (0,)), ((), ())), preferred_element_type=jnp.float32
            )
            states[head] = jnp.exp(total) * state + update
            inverse_rms = lax.rsqrt(jnp.mean(attended * attended, axis=-1, keepdims=True) + 1e-06)
            results.append((attended * inverse_rms).astype(jnp.bfloat16))
        mixed = jnp.concatenate(results, axis=1).reshape(2, BLOCK // 2, 2 * DH)
        out_ref[2 * step : 2 * step + 2] = mixed


def attend(chunks, core, kept, got, row, column):
    vmem = pl.BlockSpec(memory_space=pltpu.VMEM)
    smem = pl.BlockSpec(memory_space=pltpu.SMEM)
    return pl.pallas_call(
        attend_kernel,
        out_shape=jax.ShapeDtypeStruct((16, 128, 256), jnp.bfloat16),
        in_specs=[smem, smem] + [vmem] * (2 * len(BATCHES) + 2),
        out_specs=vmem,
        scratch_shapes=[pltpu.VMEM((16, 2, 64, 768), jnp.bfloat16)],
        compiler_params=pltpu.CompilerParams(vmem_limit_bytes=24 << 20),
        cost_estimate=pl.CostEstimate(
            flops=16 * 50_331_648, bytes_accessed=4 << 20, transcendentals=0
        ),
        name="attend",
    )(chunks, core, *kept, *got, row, column)


def shards(tokens, query_weight, key_weight, value_weight, log_decay):
    core, half, z = lax.axis_index("c"), lax.axis_index("xh"), lax.axis_index("z")
    on_place = core == half
    weight = gather_weight(jnp.concatenate((query_weight, key_weight, value_weight), axis=1))
    normed = normalize_rows(tokens[0]).reshape(2, 64, 4096)
    kept = lax.dynamic_index_in_dim(normed, core, 0, keepdims=False)
    given = lax.dynamic_index_in_dim(normed, 1 - core, 0, keepdims=False)
    got = swap_core(given)
    near = jnp.where(on_place, kept, got)
    far = swap_half(jnp.where(on_place, got, kept))

    decay = swap_roles(log_decay[0])
    g = jnp.cumsum(decay.reshape(2, 8, BLOCK), axis=-1)
    row, column = g.transpose(1, 0, 2), g.transpose(1, 2, 0)

    held = {}
    for kind, mine in enumerate((near, far)):
        held[kind, 0] = (mine,)
        up = down = mine
        for distance in range(1, 4):
            up, down = ring_z(up, 1), ring_z(down, -1)
            held[kind, distance], held[kind, 8 - distance] = (up,), (down,)
        held[kind, 4] = (ring_z(up[:32], 1), ring_z(down[32:], -1))
    place = core.astype(jnp.int32).reshape(1)
    early, late = ([p for at in SLOTS[i:j] for p in held[at]] for i, j in BATCHES)
    for_other, for_me = project(place, early, weight, True)
    late_mine, late_other = project(
        place, late + [swap_core(piece) for piece in late], weight, False
    )
    mine, others = (for_me, late_mine), (swap_core(for_other), late_other)

    chunks = jnp.stack(
        [(half + kind) % 2 * 8 + jnp.mod(z - step, 8) for kind, step in SLOTS]
    ).astype(jnp.int32)
    mixed = attend(chunks, place, mine, others, row, column)

    spread = lax.all_to_all(mixed, ("xh", "z"), split_axis=0, concat_axis=0, tiled=True)
    spread = spread.reshape(2, 8, 128, 256)
    kept = lax.dynamic_index_in_dim(spread, core, 0, keepdims=False)
    got = swap_core(lax.dynamic_index_in_dim(spread, 1 - core, 0, keepdims=False))
    first = jnp.where(core == 0, kept, got)
    second = jnp.where(core == 0, got, kept)
    out = jnp.concatenate((first, second)).transpose(1, 0, 2)
    return out.reshape(1, 128, 4096)


def solution(mesh):
    inner = Mesh(mesh.devices.reshape(SHAPE), NAMES)
    rows, lanes = ("y", "xl", "c"), ("xh", "z")
    placed = (
        P(rows, lanes, None),
        P(rows, lanes),
        P(rows, lanes),
        P(rows, lanes),
        P(rows, lanes, None),
    )
    return jax.shard_map(
        shards, mesh=inner, in_specs=placed, out_specs=P(rows, lanes, None), check_vma=False
    )
```

```python
import functools

import jax
import jax.numpy as jnp
from jax import lax
from jax.experimental import pallas as pl
from jax.experimental.pallas import tpu as pltpu
from jax.sharding import Mesh, PartitionSpec as P

BLOCK = 256
DH = 128
SHAPE = (4, 2, 2, 2, 8)
NAMES = ("y", "xl", "c", "xh", "z")


def swap_core(value):
    return lax.ppermute(value, "c", [(0, 1), (1, 0)])


def swap_half(value):
    return lax.ppermute(value, "xh", [(0, 1), (1, 0)])


def swap_roles(value):
    return lax.ppermute(value, ("c", "xh"), [(0, 0), (1, 2), (2, 1), (3, 3)])


def normalize_rows(token_rows):
    values_f = token_rows.astype(jnp.float32)
    inverse_rms = lax.rsqrt(jnp.mean(values_f * values_f, axis=-1, keepdims=True) + 1e-05)
    return (values_f * inverse_rms).astype(jnp.bfloat16)


def ring_z(value, step):
    return lax.ppermute(value, "z", [(i, (i + step) % 8) for i in range(8)])


def after(value, *others):
    anywhere = pl.BlockSpec(memory_space=pl.ANY)
    return pl.pallas_call(
        lambda *refs: None,
        out_shape=jax.ShapeDtypeStruct(value.shape, value.dtype),
        in_specs=[anywhere] * (1 + len(others)),
        out_specs=anywhere,
        input_output_aliases={0: 0},
        name="after",
    )(value, *others)


def gather_weight(weight):
    order = [
        ((y * 2 + xl) * 2 + core) * 2 + xh
        for y in range(4)
        for xh in range(2)
        for xl in range(2)
        for core in range(2)
    ]
    whole = lax.all_gather(
        weight, ("y", "xl", "c", "xh"), axis=0, tiled=False, axis_index_groups=[order]
    )
    return whole.reshape(4, 2, 1024, weight.shape[1])


SLOTS = (
    [(0, 0), (1, 0), (0, 1), (0, 7), (0, 2), (0, 6), (1, 1), (1, 7)]
    + [(0, 3), (0, 5), (1, 2), (1, 6), (1, 3), (1, 5)]
    + [(0, 4), (1, 4)]
)
BATCHES = ((0, 8), (8, 14), (14, 16))


def project_kernel(count, core_ref, *refs):
    pieces, weight_ref = refs[:count], refs[count]
    given_ref, kept_ref = refs[count + 1 :]
    group, part = pl.program_id(0), pl.program_id(1)
    rows = jnp.concatenate([piece[...] for piece in pieces], axis=0)
    weight = weight_ref[:, 0].reshape(4096, 256)
    product = jnp.dot(rows, weight, preferred_element_type=jnp.float32)
    gated = product / (1.0 + jnp.exp(-product))
    result = jnp.where(part < 2, gated, product).astype(jnp.bfloat16).reshape(kept_ref.shape)

    @pl.when(group == 0)
    def _():
        given_ref[...] = result

    @pl.when(group == 1)
    def _():
        kept_ref[...] = result


def project(core, pieces, weight):
    rows = sum(piece.shape[0] for piece in pieces)
    width = weight.shape[3]
    slots = rows // 64
    out = jax.ShapeDtypeStruct((slots, 64, width), jnp.bfloat16)

    def columns(g, p, core):
        return 0, g * core[0] + (1 - g) * (1 - core[0]), 0, p

    return pl.pallas_call(
        functools.partial(project_kernel, len(pieces)),
        out_shape=(out, out),
        grid_spec=pltpu.PrefetchScalarGridSpec(
            num_scalar_prefetch=1,
            grid=(2, 3),
            in_specs=[pl.BlockSpec(piece.shape, lambda g, p, core: (0, 0)) for piece in pieces]
            + [pl.BlockSpec((4, 1, 1024, 256), columns)],
            out_specs=[
                pl.BlockSpec((slots, 64, 256), lambda g, p, core: (0, 0, (1 - g) * p + g * 2)),
                pl.BlockSpec((slots, 64, 256), lambda g, p, core: (0, 0, g * p)),
            ],
        ),
        compiler_params=pltpu.CompilerParams(vmem_limit_bytes=58 << 20),
        cost_estimate=pl.CostEstimate(
            flops=4 * rows * 4096 * width,
            bytes_accessed=2 * rows * 8192 + (12 << 20),
            transcendentals=0,
        ),
        name="project",
    )(core, *pieces, weight)


def finish_kernel(chunk_ref, core_ref, one, two, three, four, weight_ref, *refs):
    count = len(BATCHES) - 1
    kept, got = refs[:count], refs[count : 2 * count]
    row_ref, column_ref, out_ref, new_ref, all_ref, sems = refs[2 * count :]
    part = pl.program_id(0)
    core = core_ref[0]
    copies = []
    for batch, (first, last) in enumerate(BATCHES[:count]):
        for slot in range(first, last):
            for place, source in enumerate((kept, got)):
                half = core if place == 0 else 1 - core
                copies.append(
                    pltpu.make_async_copy(
                        source[batch].at[slot - first],
                        all_ref.at[chunk_ref[slot], half],
                        sems.at[2 * slot + place],
                    )
                )

    @pl.when(part == 0)
    def _():
        for copy in copies:
            copy.start()

    rows = jnp.concatenate([piece[...] for piece in (one, two, three, four)], axis=0)
    weight = weight_ref[:, 0].reshape(4096, 256)
    product = jnp.dot(rows, weight, preferred_element_type=jnp.float32)
    gated = product / (1.0 + jnp.exp(-product))
    result = jnp.where(part < 2, gated, product).astype(jnp.bfloat16)
    new_ref[:, :, pl.ds(pl.multiple_of(part * 256, 256), 256)] = result.reshape(-1, 64, 256)

    @pl.when(part == 2)
    def _():
        for copy in copies:
            copy.wait()
        first, last = BATCHES[-1]
        for i in range(last - first):
            all_ref[chunk_ref[first + i], core] = new_ref[i]
            all_ref[chunk_ref[first + i], 1 - core] = new_ref[last - first + i]
        attend(row_ref, column_ref, out_ref, all_ref)


def attend(row_ref, column_ref, out_ref, all_ref):
    later = lax.broadcasted_iota(jnp.int32, (BLOCK, BLOCK), 0)
    earlier = lax.broadcasted_iota(jnp.int32, (BLOCK, BLOCK), 1)
    causal = later >= earlier
    states = [jnp.zeros((DH, DH), jnp.float32)] * 2
    for step in range(8):
        rows = all_ref[2 * step : 2 * step + 2].reshape(BLOCK, 768)
        results = []
        for head in range(2):
            query = rows[:, head * DH : (head + 1) * DH]
            keys = rows[:, 256 + head * DH : 256 + (head + 1) * DH]
            values = rows[:, 512 + head * DH : 512 + (head + 1) * DH]
            g_row = row_ref[step, head : head + 1, :]
            g_column = column_ref[step, :, head : head + 1]
            total = g_row[:, BLOCK - 1 :]
            scores = lax.dot_general(
                query, keys, (((1,), (1,)), ((), ())), preferred_element_type=jnp.float32
            )
            weights = jnp.exp(jnp.where(causal, g_column - g_row, -jnp.inf))
            weighted = (scores * weights).astype(jnp.bfloat16)
            scaled_query = (query.astype(jnp.float32) * jnp.exp(g_column)).astype(jnp.bfloat16)
            state = states[head]
            attended = jnp.dot(weighted, values, preferred_element_type=jnp.float32) + jnp.dot(
                scaled_query, state.astype(jnp.bfloat16), preferred_element_type=jnp.float32
            )
            faded_keys = (keys.astype(jnp.float32) * jnp.exp(total - g_column)).astype(jnp.bfloat16)
            update = lax.dot_general(
                faded_keys, values, (((0,), (0,)), ((), ())), preferred_element_type=jnp.float32
            )
            states[head] = jnp.exp(total) * state + update
            inverse_rms = lax.rsqrt(jnp.mean(attended * attended, axis=-1, keepdims=True) + 1e-06)
            results.append((attended * inverse_rms).astype(jnp.bfloat16))
        mixed = jnp.concatenate(results, axis=1).reshape(2, BLOCK // 2, 2 * DH)
        out_ref[2 * step : 2 * step + 2] = mixed


def finish(chunks, core, pieces, weight, kept, got, row, column):
    width = weight.shape[3]
    anywhere = pl.BlockSpec(memory_space=pl.ANY)

    def whole(array):
        return pl.BlockSpec(array.shape, lambda p, chunks, core: (0,) * array.ndim)

    return pl.pallas_call(
        finish_kernel,
        out_shape=jax.ShapeDtypeStruct((16, 128, 256), jnp.bfloat16),
        grid_spec=pltpu.PrefetchScalarGridSpec(
            num_scalar_prefetch=2,
            grid=(3,),
            in_specs=[whole(piece) for piece in pieces]
            + [pl.BlockSpec((4, 1, 1024, 256), lambda p, chunks, core: (0, core[0], 0, p))]
            + [anywhere] * (len(kept) + len(got))
            + [whole(row), whole(column)],
            out_specs=pl.BlockSpec((16, 128, 256), lambda p, chunks, core: (0, 0, 0)),
            scratch_shapes=[
                pltpu.VMEM((4, 64, width), jnp.bfloat16),
                pltpu.VMEM((16, 2, 64, width), jnp.bfloat16),
                pltpu.SemaphoreType.DMA((2 * BATCHES[-1][0],)),
            ],
        ),
        compiler_params=pltpu.CompilerParams(vmem_limit_bytes=58 << 20),
        cost_estimate=pl.CostEstimate(
            flops=2 * 256 * 4096 * width + 16 * 50_331_648,
            bytes_accessed=12 << 20,
            transcendentals=0,
        ),
        name="finish",
    )(chunks, core, *pieces, weight, *kept, *got, row, column)


def shards(tokens, query_weight, key_weight, value_weight, log_decay):
    core, half, z = lax.axis_index("c"), lax.axis_index("xh"), lax.axis_index("z")
    on_place = core == half
    weight = gather_weight(jnp.concatenate((query_weight, key_weight, value_weight), axis=1))
    normed = normalize_rows(tokens[0]).reshape(2, 64, 4096)
    kept = lax.dynamic_index_in_dim(normed, core, 0, keepdims=False)
    given = lax.dynamic_index_in_dim(normed, 1 - core, 0, keepdims=False)
    got = swap_core(given)
    near = jnp.where(on_place, kept, got)
    far = swap_half(jnp.where(on_place, got, kept))

    decay = swap_roles(log_decay[0])
    g = jnp.cumsum(decay.reshape(2, 8, BLOCK), axis=-1)
    row, column = g.transpose(1, 0, 2), g.transpose(1, 2, 0)

    chunks = jnp.stack(
        [(half + kind) % 2 * 8 + jnp.mod(z - step, 8) for kind, step in SLOTS]
    ).astype(jnp.int32)
    place = after(core.astype(jnp.int32).reshape(1), chunks, row, column)
    held = {}
    for kind, mine in enumerate((near, far)):
        held[kind, 0] = (mine,)
        up = down = mine
        for distance in range(1, 4):
            up, down = ring_z(up, 1), ring_z(down, -1)
            held[kind, distance], held[kind, 8 - distance] = (up,), (down,)
    first = [p for at in SLOTS[slice(*BATCHES[0])] for p in held[at]]
    first_other, first_me = project(place, first, weight)
    ends = [after(*held[0, 3], first_other), after(*held[1, 5], first_other)]
    held[0, 3], held[1, 5] = ends[:1], ends[1:]
    last = [ring_z(ends[0], 1), ring_z(ends[1], -1)]
    second = [p for at in SLOTS[slice(*BATCHES[1])] for p in held[at]]
    second_other, second_me = project(place, second, weight)
    swapped = [swap_core(piece) for piece in last]
    first_other = swap_core(after(first_other, second_me))
    others = (first_other, swap_core(second_other))
    mixed = finish(
        chunks, place, last + swapped, weight, (first_me, second_me), others, row, column
    )

    spread = lax.all_to_all(mixed, ("xh", "z"), split_axis=0, concat_axis=0, tiled=True)
    spread = spread.reshape(2, 8, 128, 256)
    kept = lax.dynamic_index_in_dim(spread, core, 0, keepdims=False)
    got = swap_core(lax.dynamic_index_in_dim(spread, 1 - core, 0, keepdims=False))
    first = jnp.where(core == 0, kept, got)
    second = jnp.where(core == 0, got, kept)
    out = jnp.concatenate((first, second)).transpose(1, 0, 2)
    return out.reshape(1, 128, 4096)


def solution(mesh):
    inner = Mesh(mesh.devices.reshape(SHAPE), NAMES)
    rows, lanes = ("y", "xl", "c"), ("xh", "z")
    placed = (
        P(rows, lanes, None),
        P(rows, lanes),
        P(rows, lanes),
        P(rows, lanes),
        P(rows, lanes, None),
    )
    return jax.shard_map(
        shards, mesh=inner, in_specs=placed, out_specs=P(rows, lanes, None), check_vma=False
    )
```

```python
import functools

import jax
import jax.numpy as jnp
from jax import lax
from jax.experimental import pallas as pl
from jax.experimental.pallas import tpu as pltpu
from jax.sharding import Mesh, PartitionSpec as P

BLOCK = 256
DH = 128
SHAPE = (4, 2, 2, 2, 8)
NAMES = ("y", "xl", "c", "xh", "z")


def swap_core(value):
    return lax.ppermute(value, "c", [(0, 1), (1, 0)])


def swap_half(value):
    return lax.ppermute(value, "xh", [(0, 1), (1, 0)])


def swap_roles(value):
    return lax.ppermute(value, ("c", "xh"), [(0, 0), (1, 2), (2, 1), (3, 3)])


def normalize_rows(token_rows):
    values_f = token_rows.astype(jnp.float32)
    inverse_rms = lax.rsqrt(jnp.mean(values_f * values_f, axis=-1, keepdims=True) + 1e-05)
    return (values_f * inverse_rms).astype(jnp.bfloat16)


def ring_z(value, step):
    return lax.ppermute(value, "z", [(i, (i + step) % 8) for i in range(8)])


def after(value, *others):
    anywhere = pl.BlockSpec(memory_space=pl.ANY)
    return pl.pallas_call(
        lambda *refs: None,
        out_shape=jax.ShapeDtypeStruct(value.shape, value.dtype),
        in_specs=[anywhere] * (1 + len(others)),
        out_specs=anywhere,
        input_output_aliases={0: 0},
        name="after",
    )(value, *others)


def gather_weight(weight):
    order = [
        ((y * 2 + xl) * 2 + core) * 2 + xh
        for y in range(4)
        for xh in range(2)
        for xl in range(2)
        for core in range(2)
    ]
    whole = lax.all_gather(
        weight, ("y", "xl", "c", "xh"), axis=0, tiled=False, axis_index_groups=[order]
    )
    return whole.reshape(4, 2, 1024, weight.shape[1])


SLOTS = (
    [(0, 0), (1, 0), (0, 1), (0, 7), (0, 2), (0, 6), (1, 1), (1, 7)]
    + [(0, 3), (0, 5), (1, 2), (1, 6), (1, 3), (1, 5)]
    + [(0, 4), (1, 4)]
)
BATCHES = ((0, 5), (5, 14), (14, 16))


def project_kernel(count, core_ref, *refs):
    pieces, weight_ref = refs[:count], refs[count]
    given_ref, kept_ref = refs[count + 1 :]
    group, part = pl.program_id(0), pl.program_id(1)
    rows = jnp.concatenate([piece[...] for piece in pieces], axis=0)
    weight = weight_ref[:, 0].reshape(4096, 256)
    product = jnp.dot(rows, weight, preferred_element_type=jnp.float32)
    gated = product / (1.0 + jnp.exp(-product))
    result = jnp.where(part < 2, gated, product).astype(jnp.bfloat16).reshape(kept_ref.shape)

    @pl.when(group == 0)
    def _():
        given_ref[...] = result

    @pl.when(group == 1)
    def _():
        kept_ref[...] = result


def project(core, pieces, weight):
    rows = sum(piece.shape[0] for piece in pieces)
    width = weight.shape[3]
    slots = rows // 64
    out = jax.ShapeDtypeStruct((slots, 64, width), jnp.bfloat16)

    def columns(g, p, core):
        return 0, g * core[0] + (1 - g) * (1 - core[0]), 0, p

    return pl.pallas_call(
        functools.partial(project_kernel, len(pieces)),
        out_shape=(out, out),
        grid_spec=pltpu.PrefetchScalarGridSpec(
            num_scalar_prefetch=1,
            grid=(2, 3),
            in_specs=[pl.BlockSpec(piece.shape, lambda g, p, core: (0, 0)) for piece in pieces]
            + [pl.BlockSpec((4, 1, 1024, 256), columns)],
            out_specs=[
                pl.BlockSpec((slots, 64, 256), lambda g, p, core: (0, 0, (1 - g) * p + g * 2)),
                pl.BlockSpec((slots, 64, 256), lambda g, p, core: (0, 0, g * p)),
            ],
        ),
        compiler_params=pltpu.CompilerParams(vmem_limit_bytes=58 << 20),
        cost_estimate=pl.CostEstimate(
            flops=4 * rows * 4096 * width,
            bytes_accessed=2 * rows * 8192 + (12 << 20),
            transcendentals=0,
        ),
        name="project",
    )(core, *pieces, weight)


def finish_kernel(chunk_ref, core_ref, one, two, three, four, weight_ref, *refs):
    count = len(BATCHES) - 1
    kept, got = refs[:count], refs[count : 2 * count]
    row_ref, column_ref, out_ref, new_ref, all_ref, sems = refs[2 * count :]
    part = pl.program_id(0)
    core = core_ref[0]
    copies = []
    for batch, (first, last) in enumerate(BATCHES[:count]):
        for slot in range(first, last):
            for place, source in enumerate((kept, got)):
                half = core if place == 0 else 1 - core
                copies.append(
                    pltpu.make_async_copy(
                        source[batch].at[slot - first],
                        all_ref.at[chunk_ref[slot], half],
                        sems.at[2 * slot + place],
                    )
                )

    @pl.when(part == 0)
    def _():
        for copy in copies:
            copy.start()

    rows = jnp.concatenate([piece[...] for piece in (one, two, three, four)], axis=0)
    weight = weight_ref[:, 0].reshape(4096, 256)
    product = jnp.dot(rows, weight, preferred_element_type=jnp.float32)
    gated = product / (1.0 + jnp.exp(-product))
    result = jnp.where(part < 2, gated, product).astype(jnp.bfloat16)
    new_ref[:, :, pl.ds(pl.multiple_of(part * 256, 256), 256)] = result.reshape(-1, 64, 256)

    @pl.when(part == 2)
    def _():
        for copy in copies:
            copy.wait()
        first, last = BATCHES[-1]
        for i in range(last - first):
            all_ref[chunk_ref[first + i], core] = new_ref[i]
            all_ref[chunk_ref[first + i], 1 - core] = new_ref[last - first + i]
        attend(row_ref, column_ref, out_ref, all_ref)


def attend(row_ref, column_ref, out_ref, all_ref):
    later = lax.broadcasted_iota(jnp.int32, (BLOCK, BLOCK), 0)
    earlier = lax.broadcasted_iota(jnp.int32, (BLOCK, BLOCK), 1)
    causal = later >= earlier
    states = [jnp.zeros((DH, DH), jnp.float32)] * 2
    for step in range(8):
        rows = all_ref[2 * step : 2 * step + 2].reshape(BLOCK, 768)
        results = []
        for head in range(2):
            query = rows[:, head * DH : (head + 1) * DH]
            keys = rows[:, 256 + head * DH : 256 + (head + 1) * DH]
            values = rows[:, 512 + head * DH : 512 + (head + 1) * DH]
            g_row = row_ref[step, head : head + 1, :]
            g_column = column_ref[step, :, head : head + 1]
            total = g_row[:, BLOCK - 1 :]
            scores = lax.dot_general(
                query, keys, (((1,), (1,)), ((), ())), preferred_element_type=jnp.float32
            )
            weights = jnp.exp(jnp.where(causal, g_column - g_row, -jnp.inf))
            weighted = (scores * weights).astype(jnp.bfloat16)
            scaled_query = (query.astype(jnp.float32) * jnp.exp(g_column)).astype(jnp.bfloat16)
            state = states[head]
            attended = jnp.dot(weighted, values, preferred_element_type=jnp.float32) + jnp.dot(
                scaled_query, state.astype(jnp.bfloat16), preferred_element_type=jnp.float32
            )
            faded_keys = (keys.astype(jnp.float32) * jnp.exp(total - g_column)).astype(jnp.bfloat16)
            update = lax.dot_general(
                faded_keys, values, (((0,), (0,)), ((), ())), preferred_element_type=jnp.float32
            )
            states[head] = jnp.exp(total) * state + update
            inverse_rms = lax.rsqrt(jnp.mean(attended * attended, axis=-1, keepdims=True) + 1e-06)
            results.append((attended * inverse_rms).astype(jnp.bfloat16))
        mixed = jnp.concatenate(results, axis=1).reshape(2, BLOCK // 2, 2 * DH)
        out_ref[2 * step : 2 * step + 2] = mixed


def finish(chunks, core, pieces, weight, kept, got, row, column):
    width = weight.shape[3]
    anywhere = pl.BlockSpec(memory_space=pl.ANY)

    def whole(array):
        return pl.BlockSpec(array.shape, lambda p, chunks, core: (0,) * array.ndim)

    return pl.pallas_call(
        finish_kernel,
        out_shape=jax.ShapeDtypeStruct((16, 128, 256), jnp.bfloat16),
        grid_spec=pltpu.PrefetchScalarGridSpec(
            num_scalar_prefetch=2,
            grid=(3,),
            in_specs=[whole(piece) for piece in pieces]
            + [pl.BlockSpec((4, 1, 1024, 256), lambda p, chunks, core: (0, core[0], 0, p))]
            + [anywhere] * (len(kept) + len(got))
            + [whole(row), whole(column)],
            out_specs=pl.BlockSpec((16, 128, 256), lambda p, chunks, core: (0, 0, 0)),
            scratch_shapes=[
                pltpu.VMEM((4, 64, width), jnp.bfloat16),
                pltpu.VMEM((16, 2, 64, width), jnp.bfloat16),
                pltpu.SemaphoreType.DMA((2 * BATCHES[-1][0],)),
            ],
        ),
        compiler_params=pltpu.CompilerParams(vmem_limit_bytes=58 << 20),
        cost_estimate=pl.CostEstimate(
            flops=2 * 256 * 4096 * width + 16 * 50_331_648,
            bytes_accessed=12 << 20,
            transcendentals=0,
        ),
        name="finish",
    )(chunks, core, *pieces, weight, *kept, *got, row, column)


def shards(tokens, query_weight, key_weight, value_weight, log_decay):
    core, half, z = lax.axis_index("c"), lax.axis_index("xh"), lax.axis_index("z")
    on_place = core == half
    weight = gather_weight(jnp.concatenate((query_weight, key_weight, value_weight), axis=1))
    normed = normalize_rows(tokens[0]).reshape(2, 64, 4096)
    kept = lax.dynamic_index_in_dim(normed, core, 0, keepdims=False)
    given = lax.dynamic_index_in_dim(normed, 1 - core, 0, keepdims=False)
    got = swap_core(given)
    near = jnp.where(on_place, kept, got)
    far = swap_half(jnp.where(on_place, got, kept))

    decay = swap_roles(log_decay[0])
    g = jnp.cumsum(decay.reshape(2, 8, BLOCK), axis=-1)
    row, column = g.transpose(1, 0, 2), g.transpose(1, 2, 0)

    chunks = jnp.stack(
        [(half + kind) % 2 * 8 + jnp.mod(z - step, 8) for kind, step in SLOTS]
    ).astype(jnp.int32)
    place = after(core.astype(jnp.int32).reshape(1), chunks, row, column)
    held = {}
    for kind, mine in enumerate((near, far)):
        held[kind, 0] = (mine,)
        up = down = mine
        for distance in range(1, 4):
            up, down = ring_z(up, 1), ring_z(down, -1)
            held[kind, distance], held[kind, 8 - distance] = (up,), (down,)
    first = [p for at in SLOTS[slice(*BATCHES[0])] for p in held[at]]
    first_other, first_me = project(place, first, weight)
    ends = [after(*held[0, 3], first_other), after(*held[1, 5], first_other)]
    held[0, 3], held[1, 5] = ends[:1], ends[1:]
    last = [ring_z(ends[0], 1), ring_z(ends[1], -1)]
    second = [p for at in SLOTS[slice(*BATCHES[1])] for p in held[at]]
    second_other, second_me = project(place, second, weight)
    swapped = [swap_core(piece) for piece in last]
    first_other = swap_core(after(first_other, second_me))
    others = (first_other, swap_core(second_other))
    mixed = finish(
        chunks, place, last + swapped, weight, (first_me, second_me), others, row, column
    )

    spread = lax.all_to_all(mixed, ("xh", "z"), split_axis=0, concat_axis=0, tiled=True)
    spread = spread.reshape(2, 8, 128, 256)
    kept = lax.dynamic_index_in_dim(spread, core, 0, keepdims=False)
    got = swap_core(lax.dynamic_index_in_dim(spread, 1 - core, 0, keepdims=False))
    first = jnp.where(core == 0, kept, got)
    second = jnp.where(core == 0, got, kept)
    out = jnp.concatenate((first, second)).transpose(1, 0, 2)
    return out.reshape(1, 128, 4096)


def solution(mesh):
    inner = Mesh(mesh.devices.reshape(SHAPE), NAMES)
    rows, lanes = ("y", "xl", "c"), ("xh", "z")
    placed = (
        P(rows, lanes, None),
        P(rows, lanes),
        P(rows, lanes),
        P(rows, lanes),
        P(rows, lanes, None),
    )
    return jax.shard_map(
        shards, mesh=inner, in_specs=placed, out_specs=P(rows, lanes, None), check_vma=False
    )
```

```python
import functools

import jax
import jax.numpy as jnp
from jax import lax
from jax.experimental import pallas as pl
from jax.experimental.pallas import tpu as pltpu
from jax.sharding import Mesh, PartitionSpec as P

BLOCK = 256
DH = 128
SHAPE = (4, 2, 2, 2, 8)
NAMES = ("y", "xl", "c", "xh", "z")


def swap_core(value):
    return lax.ppermute(value, "c", [(0, 1), (1, 0)])


def swap_half(value):
    return lax.ppermute(value, "xh", [(0, 1), (1, 0)])


def swap_roles(value):
    return lax.ppermute(value, ("c", "xh"), [(0, 0), (1, 2), (2, 1), (3, 3)])


def normalize_rows(token_rows):
    values_f = token_rows.astype(jnp.float32)
    inverse_rms = lax.rsqrt(jnp.mean(values_f * values_f, axis=-1, keepdims=True) + 1e-05)
    return (values_f * inverse_rms).astype(jnp.bfloat16)


def ring_z(value, step):
    return lax.ppermute(value, "z", [(i, (i + step) % 8) for i in range(8)])


def after(value, *others):
    anywhere = pl.BlockSpec(memory_space=pl.ANY)
    return pl.pallas_call(
        lambda *refs: None,
        out_shape=jax.ShapeDtypeStruct(value.shape, value.dtype),
        in_specs=[anywhere] * (1 + len(others)),
        out_specs=anywhere,
        input_output_aliases={0: 0},
        name="after",
    )(value, *others)


def gather_weight(weight):
    order = [
        ((y * 2 + xl) * 2 + core) * 2 + xh
        for y in range(4)
        for xh in range(2)
        for xl in range(2)
        for core in range(2)
    ]
    whole = lax.all_gather(
        weight, ("y", "xl", "c", "xh"), axis=0, tiled=False, axis_index_groups=[order]
    )
    return whole.reshape(4, 2, 1024, weight.shape[1])


SLOTS = (
    [(0, 0), (1, 0), (0, 1), (0, 7), (0, 2), (0, 6), (1, 1), (1, 7)]
    + [(0, 3), (0, 5), (1, 2), (1, 6), (1, 3), (1, 5)]
    + [(0, 4), (1, 4)]
)
BATCHES = ((0, 5), (5, 14), (14, 16))


def project_kernel(count, core_ref, *refs):
    pieces, weight_ref = refs[:count], refs[count]
    given_ref, kept_ref = refs[count + 1 :]
    group, part = pl.program_id(0), pl.program_id(1)
    rows = jnp.concatenate([piece[...] for piece in pieces], axis=0)
    weight = weight_ref[:, 0].reshape(4096, 256)
    product = jnp.dot(rows, weight, preferred_element_type=jnp.float32)
    gated = product / (1.0 + jnp.exp(-product))
    result = jnp.where(part < 2, gated, product).astype(jnp.bfloat16).reshape(kept_ref.shape)

    @pl.when(group == 0)
    def _():
        given_ref[...] = result

    @pl.when(group == 1)
    def _():
        kept_ref[...] = result


def project(core, pieces, weight):
    rows = sum(piece.shape[0] for piece in pieces)
    width = weight.shape[3]
    slots = rows // 64
    out = jax.ShapeDtypeStruct((slots, 64, width), jnp.bfloat16)

    def columns(g, p, core):
        return 0, g * core[0] + (1 - g) * (1 - core[0]), 0, p

    return pl.pallas_call(
        functools.partial(project_kernel, len(pieces)),
        out_shape=(out, out),
        grid_spec=pltpu.PrefetchScalarGridSpec(
            num_scalar_prefetch=1,
            grid=(2, 3),
            in_specs=[pl.BlockSpec(piece.shape, lambda g, p, core: (0, 0)) for piece in pieces]
            + [pl.BlockSpec((4, 1, 1024, 256), columns)],
            out_specs=[
                pl.BlockSpec((slots, 64, 256), lambda g, p, core: (0, 0, (1 - g) * p + g * 2)),
                pl.BlockSpec((slots, 64, 256), lambda g, p, core: (0, 0, g * p)),
            ],
        ),
        compiler_params=pltpu.CompilerParams(vmem_limit_bytes=58 << 20),
        cost_estimate=pl.CostEstimate(
            flops=4 * rows * 4096 * width,
            bytes_accessed=2 * rows * 8192 + (12 << 20),
            transcendentals=0,
        ),
        name="project",
    )(core, *pieces, weight)


def finish_kernel(chunk_ref, core_ref, one, two, three, four, weight_ref, *refs):
    count = len(BATCHES) - 1
    kept, got = refs[:count], refs[count : 2 * count]
    row_ref, column_ref, out_ref, new_ref, all_ref, sems = refs[2 * count :]
    part = pl.program_id(0)
    core = core_ref[0]
    copies = []
    for batch, (first, last) in enumerate(BATCHES[:count]):
        for slot in range(first, last):
            for place, source in enumerate((kept, got)):
                half = core if place == 0 else 1 - core
                copies.append(
                    pltpu.make_async_copy(
                        source[batch].at[slot - first],
                        all_ref.at[chunk_ref[slot], half],
                        sems.at[2 * slot + place],
                    )
                )

    @pl.when(part == 0)
    def _():
        for copy in copies:
            copy.start()

    rows = jnp.concatenate([piece[...] for piece in (one, two, three, four)], axis=0)
    weight = weight_ref[:, 0].reshape(4096, 256)
    product = jnp.dot(rows, weight, preferred_element_type=jnp.float32)
    gated = product / (1.0 + jnp.exp(-product))
    result = jnp.where(part < 2, gated, product).astype(jnp.bfloat16)
    new_ref[:, :, pl.ds(pl.multiple_of(part * 256, 256), 256)] = result.reshape(-1, 64, 256)

    @pl.when(part == 2)
    def _():
        for copy in copies:
            copy.wait()
        first, last = BATCHES[-1]
        for i in range(last - first):
            all_ref[chunk_ref[first + i], core] = new_ref[i]
            all_ref[chunk_ref[first + i], 1 - core] = new_ref[last - first + i]
        attend(row_ref, column_ref, out_ref, all_ref)


def attend(row_ref, column_ref, out_ref, all_ref):
    later = lax.broadcasted_iota(jnp.int32, (BLOCK, BLOCK), 0)
    earlier = lax.broadcasted_iota(jnp.int32, (BLOCK, BLOCK), 1)
    causal = later >= earlier
    states = [jnp.zeros((DH, DH), jnp.float32)] * 2
    for step in range(8):
        rows = all_ref[2 * step : 2 * step + 2].reshape(BLOCK, 768)
        results, queries, locals_, updates = [], [], [], []
        for head in range(2):
            query = rows[:, head * DH : (head + 1) * DH]
            keys = rows[:, 256 + head * DH : 256 + (head + 1) * DH]
            values = rows[:, 512 + head * DH : 512 + (head + 1) * DH]
            g_row = row_ref[step, head : head + 1, :]
            g_column = column_ref[step, :, head : head + 1]
            total = g_row[:, BLOCK - 1 :]
            scores = lax.dot_general(
                query, keys, (((1,), (1,)), ((), ())), preferred_element_type=jnp.float32
            )
            weights = jnp.exp(jnp.where(causal, g_column - g_row, -jnp.inf))
            weighted = (scores * weights).astype(jnp.bfloat16)
            scaled_query = (query.astype(jnp.float32) * jnp.exp(g_column)).astype(jnp.bfloat16)
            queries.append(scaled_query)
            local = jnp.dot(weighted, values, preferred_element_type=jnp.float32)
            faded_keys = (keys.astype(jnp.float32) * jnp.exp(total - g_column)).astype(jnp.bfloat16)
            update = lax.dot_general(
                faded_keys, values, (((0,), (0,)), ((), ())), preferred_element_type=jnp.float32
            )
            locals_.append(local)
            updates.append(jnp.exp(total) * states[head] + update)
        zero = jnp.zeros((DH, DH), jnp.bfloat16)
        both = jnp.concatenate(
            (
                jnp.concatenate((states[0].astype(jnp.bfloat16), zero), axis=1),
                jnp.concatenate((zero, states[1].astype(jnp.bfloat16)), axis=1),
            ),
            axis=0,
        )
        carried = jnp.dot(
            jnp.concatenate(queries, axis=1), both, preferred_element_type=jnp.float32
        )
        states = updates
        for head in range(2):
            attended = locals_[head] + carried[:, head * DH : (head + 1) * DH]
            inverse_rms = lax.rsqrt(jnp.mean(attended * attended, axis=-1, keepdims=True) + 1e-06)
            results.append((attended * inverse_rms).astype(jnp.bfloat16))
        mixed = jnp.concatenate(results, axis=1).reshape(2, BLOCK // 2, 2 * DH)
        out_ref[2 * step : 2 * step + 2] = mixed


def finish(chunks, core, pieces, weight, kept, got, row, column):
    width = weight.shape[3]
    anywhere = pl.BlockSpec(memory_space=pl.ANY)

    def whole(array):
        return pl.BlockSpec(array.shape, lambda p, chunks, core: (0,) * array.ndim)

    return pl.pallas_call(
        finish_kernel,
        out_shape=jax.ShapeDtypeStruct((16, 128, 256), jnp.bfloat16),
        grid_spec=pltpu.PrefetchScalarGridSpec(
            num_scalar_prefetch=2,
            grid=(3,),
            in_specs=[whole(piece) for piece in pieces]
            + [pl.BlockSpec((4, 1, 1024, 256), lambda p, chunks, core: (0, core[0], 0, p))]
            + [anywhere] * (len(kept) + len(got))
            + [whole(row), whole(column)],
            out_specs=pl.BlockSpec((16, 128, 256), lambda p, chunks, core: (0, 0, 0)),
            scratch_shapes=[
                pltpu.VMEM((4, 64, width), jnp.bfloat16),
                pltpu.VMEM((16, 2, 64, width), jnp.bfloat16),
                pltpu.SemaphoreType.DMA((2 * BATCHES[-1][0],)),
            ],
        ),
        compiler_params=pltpu.CompilerParams(vmem_limit_bytes=58 << 20),
        cost_estimate=pl.CostEstimate(
            flops=2 * 256 * 4096 * width + 16 * 50_331_648,
            bytes_accessed=12 << 20,
            transcendentals=0,
        ),
        name="finish",
    )(chunks, core, *pieces, weight, *kept, *got, row, column)


def shards(tokens, query_weight, key_weight, value_weight, log_decay):
    core, half, z = lax.axis_index("c"), lax.axis_index("xh"), lax.axis_index("z")
    on_place = core == half
    weight = gather_weight(jnp.concatenate((query_weight, key_weight, value_weight), axis=1))
    normed = normalize_rows(tokens[0]).reshape(2, 64, 4096)
    kept = lax.dynamic_index_in_dim(normed, core, 0, keepdims=False)
    given = lax.dynamic_index_in_dim(normed, 1 - core, 0, keepdims=False)
    got = swap_core(given)
    near = jnp.where(on_place, kept, got)
    far = swap_half(jnp.where(on_place, got, kept))

    decay = swap_roles(log_decay[0])
    g = jnp.cumsum(decay.reshape(2, 8, BLOCK), axis=-1)
    row, column = g.transpose(1, 0, 2), g.transpose(1, 2, 0)

    chunks = jnp.stack(
        [(half + kind) % 2 * 8 + jnp.mod(z - step, 8) for kind, step in SLOTS]
    ).astype(jnp.int32)
    place = after(core.astype(jnp.int32).reshape(1), chunks, row, column)
    held = {}
    for kind, mine in enumerate((near, far)):
        held[kind, 0] = (mine,)
        up = down = mine
        for distance in range(1, 4):
            up, down = ring_z(up, 1), ring_z(down, -1)
            held[kind, distance], held[kind, 8 - distance] = (up,), (down,)
    first = [p for at in SLOTS[slice(*BATCHES[0])] for p in held[at]]
    first_other, first_me = project(place, first, weight)
    ends = [after(*held[0, 3], first_other), after(*held[1, 5], first_other)]
    held[0, 3], held[1, 5] = ends[:1], ends[1:]
    last = [ring_z(ends[0], 1), ring_z(ends[1], -1)]
    second = [p for at in SLOTS[slice(*BATCHES[1])] for p in held[at]]
    second_other, second_me = project(place, second, weight)
    swapped = [swap_core(piece) for piece in last]
    first_other = swap_core(after(first_other, second_me))
    others = (first_other, swap_core(second_other))
    mixed = finish(
        chunks, place, last + swapped, weight, (first_me, second_me), others, row, column
    )

    spread = lax.all_to_all(mixed, ("xh", "z"), split_axis=0, concat_axis=0, tiled=True)
    spread = spread.reshape(2, 8, 128, 256)
    kept = lax.dynamic_index_in_dim(spread, core, 0, keepdims=False)
    got = swap_core(lax.dynamic_index_in_dim(spread, 1 - core, 0, keepdims=False))
    first = jnp.where(core == 0, kept, got)
    second = jnp.where(core == 0, got, kept)
    out = jnp.concatenate((first, second)).transpose(1, 0, 2)
    return out.reshape(1, 128, 4096)


def solution(mesh):
    inner = Mesh(mesh.devices.reshape(SHAPE), NAMES)
    rows, lanes = ("y", "xl", "c"), ("xh", "z")
    placed = (
        P(rows, lanes, None),
        P(rows, lanes),
        P(rows, lanes),
        P(rows, lanes),
        P(rows, lanes, None),
    )
    return jax.shard_map(
        shards, mesh=inner, in_specs=placed, out_specs=P(rows, lanes, None), check_vma=False
    )
```
